32 devices in a mesh: groups: 2 (over x), owner: 4 (over y, core), path: 4 (over z).
Axes of the slice: x: 2, y: 2, z: 4, core: 2. Of those that a mesh axis runs over, the one named last changes fastest.
Arguments:
- sensitivity: bfloat16 [32768, 2048], P(('groups', 'owner', 'path')), parts along dimension 0, may hold values from -0.03125 to 0.03125
- present_trade_value: float32 [32768], P(('groups', 'owner', 'path')), parts along dimension 0, may hold values from -2.5 to 2.5
- trade_set_owner: int32 [32768, 1], P(('groups', 'owner', 'path')), parts along dimension 0, may hold values from 0 to 3; in each aligned block of 1024 rows (0 to 1023, 1024 to 2047, ...) at most 1024 rows name the same one
- trade_local_set: int32 [32768], P(('groups', 'owner', 'path')), parts along dimension 0, may hold values from 0 to 255
- shocks: bfloat16 [256, 4, 2048], P(('groups', 'path')), parts along dimension 0, may hold values from -6 to 6
- collateral_of_set: int32 [2048], P(('groups', 'owner')), parts along dimension 0, may hold values from 0 to 31
- collateral_posted: float32 [64], P('groups'), parts along dimension 0, may hold values from 0.3 to 3
- discount: float32 [8], P('groups'), parts along dimension 0, may hold values from 0.5 to 1
Outputs:
- exposure_paths: float32 [2048, 512], P(('groups', 'owner'), 'path'), parts along dimension 0
- expected_exposure: float32 [2048, 4], P(('groups', 'owner')), parts along dimension 0
The draws below stay inside these ranges and needn't reach their ends.
There are 2 independent parts, one for each index of `groups`. The reference program is written for one: setup_inputs(seed, part) draws one part's arguments, and reference() takes and returns one part's arrays. A program takes and returns all parts, laid end to end along the dimension named above; each array names one. Nothing has to cross between parts.
Inputs may be any that keep to these rules, and one draw needn't show every extreme that they name: `trade_set_owner`: within the trades of one device at most 1024 name one owner, a bound that some block reaches of them.
All inputs are finite; a program needn't handle non-finite values.
Results may differ from the reference program's by a relative error of at most 0.0035.
Values may be sent and summed in bfloat16 or wider, within the bound.
A program may use at most 64 MiB of HBM per device.

```python
import math
import jax
import jax.numpy as jnp
import numpy as np
from jax import lax

F = 2048
S = 4
TR_DEV = 1024
SETS_DEV = 256
COLLATERAL_SETS = 32
TRADES = 16384
P_SIZE = 128
NETTING_TOTAL = 1024
CAP = 1024
N_OWNER = 4
N_PATH = 4


def touch_ends(drawn, key, least, top_value):
    dims = drawn.shape
    place = [jax.random.randint(jax.random.fold_in(key, axis), (), 0, dims[axis]) for axis in range(len(dims))]
    drawn = drawn.at[tuple(place)].set(least)
    longest = dims.index(max(dims))
    place[longest] = (place[longest] + 1) % dims[longest]
    return drawn.at[tuple(place)].set(top_value)


def level_of(key, shape, split, smallest, high):
    loudness = 1.0
    for position, shards_of in split:
        heights = jax.random.uniform(jax.random.fold_in(jax.random.fold_in(key, 6), position), (shards_of,), jnp.float32, smallest / len(split), high / len(split))
        loudness = loudness * jnp.repeat(jnp.exp(heights), shape[position] // shards_of).reshape((-1,) + (1,) * (len(shape) - 1 - position))
    return loudness


def shared_out(key, own, number, rows, count, top, limit, lean):
    sequence = jax.random.permutation(key, count)
    crowded, ordinary = shares(count, rows * top, limit, lean, True), shares(count, rows * top, limit, lean, False)
    places = jnp.arange(count)

    def named(tallies, rotation):
        used = int((tallies > 0).sum())
        fixed = max(1, used // 4)
        shifted = fixed + (places - fixed + rotation * (used - fixed)) % max(1, count - fixed)
        return jnp.zeros((count,), jnp.int32).at[sequence[jnp.where(places < fixed, places, shifted)]].set(jnp.asarray(tallies, jnp.int32))

    tallies = jnp.where(number % 4 == 0, named(crowded, number // 4), named(ordinary, number - number // 4 - 1))
    mixed = jax.random.permutation(jax.random.fold_in(own, 3), count)
    donor, taker = mixed[0:count // 2 * 2:2], mixed[1:count // 2 * 2:2]
    margin = jnp.minimum(tallies[donor] - 1, limit - tallies[taker]) // 2
    margin = jnp.where((donor == sequence[0]) | (taker == sequence[0]) | (tallies[taker] == 0), 0, jnp.maximum(margin, 0))
    shifted = jax.random.randint(jax.random.fold_in(own, 4), (count // 2,), 0, 1 << 20) % (margin + 1)
    tallies = tallies.at[donor].add(-shifted).at[taker].add(shifted)
    members = jnp.searchsorted(jnp.cumsum(tallies), jnp.arange(rows * top), side="right").astype(jnp.int32)
    listing = members.reshape(top, rows).T
    listing = listing[jax.random.permutation(jax.random.fold_in(own, 1), rows)]
    rotation = jax.random.randint(jax.random.fold_in(own, 2), (rows, 1), 0, top)
    return jnp.take_along_axis(listing, (jnp.arange(top)[None, :] + rotation) % top, axis=1)


def shares(number_of, total, most, skew, full):
    weights = [(1 << 20) // math.isqrt(standing ** skew) + 1 for standing in range(1, number_of + 1)]
    largest = most if full else min(most, max(-(-total // number_of), total * weights[0] // sum(weights)))
    least = 1 if total - largest >= number_of - 1 else 0
    holding, surplus = [largest] + [least] * (number_of - 1), total - largest - least * (number_of - 1)
    while surplus > 0:
        free = [i for i in range(1, number_of) if holding[i] < largest] or [i for i in range(1, number_of) if holding[i] < most]
        whole, remaining = sum([weights[i] for i in free]), surplus
        for i in free:
            extra = min(most - holding[i], max(1, remaining * weights[i] // whole), surplus)
            holding[i] = holding[i] + extra
            surplus = surplus - extra
    return np.array(holding)


def scatter_about(rng, extent, scale, bound, split=(), dtype=jnp.bfloat16):
    gain = level_of(rng, extent, split, -0.22, 0.18) if split else 1.0
    result = jax.random.normal(rng, extent, jnp.float32) * scale * gain
    return jnp.minimum(jnp.maximum(result, -bound), bound).astype(dtype)


def setup_inputs(seed: int = 0, part: int = 0) -> dict:
    keys = jax.random.split(jax.random.key(seed), 9)
    own_keys = jax.random.split(jax.random.fold_in(keys[8], part), 9)
    sensitivity = scatter_about(own_keys[0], (TRADES, F), (F * TR_DEV * N_PATH // SETS_DEV) ** -0.5, 0.03125, ((0, 16),))
    present_trade_value = scatter_about(own_keys[1], (TRADES,), (0.7 * SETS_DEV ** 0.5 * (TR_DEV * N_PATH) ** -0.5), 2.5, ((0, 16),), jnp.float32)
    trade_set_owner_keys = jax.random.split(jax.random.fold_in(own_keys[2], 1), TRADES // TR_DEV)
    trade_set_owner_turns = jax.random.permutation(jax.random.fold_in(own_keys[2], 3), TRADES // TR_DEV)
    trade_set_owner = jax.vmap(lambda own, number: shared_out(jax.random.fold_in(own_keys[2], 2), own, number, TR_DEV, N_OWNER, 1, CAP, 2))(trade_set_owner_keys, trade_set_owner_turns).reshape((TRADES, 1))
    trade_local_set = touch_ends(jax.random.randint(own_keys[3], (TRADES,), 0, SETS_DEV), jax.random.fold_in(own_keys[3], 1), 0, SETS_DEV - 1).astype(jnp.int32)
    shocks = scatter_about(own_keys[4], (P_SIZE, S, F), 1.0, 6.0, ((0, 4),))
    collateral_of_set = touch_ends(jax.random.randint(own_keys[5], (NETTING_TOTAL,), 0, COLLATERAL_SETS), jax.random.fold_in(own_keys[5], 1), 0, COLLATERAL_SETS - 1).astype(jnp.int32)
    collateral_posted = jnp.clip(jnp.exp(jax.random.uniform(own_keys[6], (COLLATERAL_SETS,), jnp.float32, math.log(0.3), math.log(3.0))), 0.3, 3.0)
    discount = jnp.clip(jax.random.uniform(own_keys[7], (S,), jnp.float32, 0.5, 1.0), 0.5, 1.0)
    return {"sensitivity": sensitivity, "present_trade_value": present_trade_value, "trade_set_owner": trade_set_owner, "trade_local_set": trade_local_set, "shocks": shocks, "collateral_of_set": collateral_of_set, "collateral_posted": collateral_posted, "discount": discount}


def reference(sensitivity, present_trade_value, trade_set_owner, trade_local_set, shocks, collateral_of_set, collateral_posted, discount):
    flat_shocks = shocks.reshape(P_SIZE * S, F).astype(jnp.float32)
    netting_id = (trade_set_owner[:, 0] * SETS_DEV + trade_local_set).astype(jnp.int32)
    blocks = sensitivity.shape[0] // TR_DEV
    sens_blocks = sensitivity.reshape(blocks, TR_DEV, F)
    base_blocks = present_trade_value.reshape(blocks, TR_DEV)
    id_blocks = netting_id.reshape(blocks, TR_DEV)

    def accumulate(nets, item):
        sens_block, base_block, id_block = item
        values = jnp.dot(sens_block.astype(jnp.float32), flat_shocks.T, preferred_element_type=jnp.float32)
        values = (values + base_block[:, None]).astype(jnp.bfloat16).astype(jnp.float32)
        nets = nets + jax.ops.segment_sum(values, id_block, num_segments=NETTING_TOTAL)
        return nets, None

    nets, _ = lax.scan(accumulate, jnp.zeros((NETTING_TOTAL, P_SIZE * S), jnp.float32), (sens_blocks, base_blocks, id_blocks))
    floored_exposure = collateral_posted[collateral_of_set][:, None]
    exposure_paths = jnp.tile(discount, P_SIZE)[None, :] * jnp.maximum(nets - floored_exposure, 0.0)
    expected_exposure = jnp.sum(exposure_paths.reshape(NETTING_TOTAL, P_SIZE, S), axis=1) / P_SIZE
    return exposure_paths, expected_exposure
```

```python
import functools

import jax
import jax.numpy as jnp
from jax import lax
from jax.experimental import pallas as pl
from jax.experimental.pallas import tpu as pltpu
from jax.sharding import PartitionSpec as P

MESH = pl.DeviceIdType.MESH
F32, BF16 = jnp.float32, jnp.bfloat16
BY_LANES = (((1,), (1,)), ((), ()))


def kernel(
    n_owner, n_path, n_sets, steps,
    sens_hbm, shock_ref, base_ref, key_ref, cset_ref, posted_ref, disc_ref,
    exp_ref, mean_ref,
    sens, moves, base_cols, hot, tv, send1, recv1, keep2, send2, recv2, acc, send3, recv3, tot, recv4,
    load_sem, a_send, a_recv, b_send, b_recv, c_send, c_recv,
    s1_send, s1_recv, s2_send, s2_recv, s3_send, s3_recv, s4_send, s4_recv,
):
    owner, me = lax.axis_index("owner"), lax.axis_index("path")
    n_y = n_owner // 2
    y, core = owner // 2, owner % 2
    partner = owner + 1 - 2 * core
    half = n_y * n_sets
    trades, factors = sens.shape
    cols = shock_ref.shape[0]
    piece = factors // n_owner
    open_sends = []

    def device(o, p):
        return {"owner": o, "path": p}

    def across(j):
        return lax.rem(y + j, n_y)

    def along(j):
        return lax.rem(me + j, n_path)

    load = pltpu.make_async_copy(sens_hbm, sens, load_sem)
    load.start()

    barrier = pltpu.get_barrier_semaphore()
    for j in range(1, n_path):
        pl.semaphore_signal(barrier, inc=1, device_id=device(owner, along(j)), device_id_type=MESH)
    for j in range(1, n_y):
        pl.semaphore_signal(
            barrier, inc=1, device_id=device(across(j) * 2 + core, me), device_id_type=MESH
        )
    pl.semaphore_signal(barrier, inc=1, device_id=device(partner, me), device_id_type=MESH)
    pl.semaphore_wait(barrier, n_path - 1 + n_y - 1 + 1)

    low_side = me <= n_path - 1 - me
    both = jnp.where(low_side, me, n_path - 1 - me)
    order = []
    for k in range(n_path):
        swing = me - (k + 1) // 2 if k % 2 else me + k // 2
        order.append(jnp.where(k <= 2 * both, swing, jnp.where(low_side, k, n_path - 1 - k)))

    def lanes(o):
        return pl.ds(pl.multiple_of(o * piece, piece), piece)

    def copy(src, dst, send_sem, recv_sem, target):
        return pltpu.make_async_remote_copy(
            src_ref=src, dst_ref=dst, send_sem=send_sem, recv_sem=recv_sem,
            device_id=target, device_id_type=MESH,
        )

    def go(c):
        c.start()
        open_sends.append(c)

    for k in range(1, n_path):
        go(copy(
            shock_ref.at[:, lanes(owner)], moves.at[me, :, lanes(owner)],
            a_send.at[k], a_recv.at[me], device(owner, order[k]),
        ))

    def spread(k):
        q = order[k]
        mine = moves.at[q, :, lanes(owner)]
        copy(mine, mine, a_send.at[k], a_recv.at[q], device(owner, q)).wait_recv()
        for j in range(1, n_y):
            go(copy(mine, mine, b_send.at[k, j], b_recv.at[q, j],
                    device(across(j) * 2 + core, me)))
        go(copy(mine, mine, c_send.at[k, 0], c_recv.at[q, 0], device(partner, me)))

    def relay(k):
        q = order[k]
        for j in range(1, n_y):
            source = across(n_y - j) * 2 + core
            got = moves.at[q, :, lanes(source)]
            copy(got, got, b_send.at[k, j], b_recv.at[q, j], device(partner, me)).wait_recv()
            go(copy(got, got, c_send.at[k, j], c_recv.at[q, j], device(partner, me)))

    def gathered(k):
        q = order[k]
        for j in range(n_y):
            got = moves.at[q, :, lanes(across(n_y - j) * 2 + 1 - core)]
            copy(got, got, c_send.at[k, j], c_recv.at[q, j], device(partner, me)).wait_recv()

    tile = min(trades, 512)

    def values(k):
        @pl.loop(0, trades // tile)
        def _(i):
            rows = pl.ds(pl.multiple_of(i * tile, tile), tile)
            block = shock_ref[...] if k == 0 else moves[order[k]]
            out = lax.dot_general(sens[rows, :], block, BY_LANES, preferred_element_type=F32)
            tv[k, rows, :] = (out + base_cols[rows, :]).astype(BF16)

        @pl.loop(0, n_y)
        def _(i):
            rows = pl.ds(pl.multiple_of(i * n_sets, n_sets), n_sets)
            send1[k, rows, :] = jnp.dot(hot[1, rows, :], tv[k], preferred_element_type=F32)

        go(copy(send1.at[k], recv1.at[k], s1_send.at[k], s1_recv.at[k], device(partner, me)))

    def set_sums(k, yy):
        rows = pl.ds(pl.multiple_of(yy * n_sets, n_sets), n_sets)
        return jnp.dot(hot[0, rows, :], tv[k], preferred_element_type=F32) + recv1[k, rows, :]

    def cross_owner(k):
        copy(send1.at[k], recv1.at[k], s1_send.at[k], s1_recv.at[k], device(partner, me)).wait_recv()
        for j in range(1, n_y):
            send2[k, j - 1] = set_sums(k, across(j)).astype(BF16)
            go(copy(send2.at[k, j - 1], recv2.at[k, j - 1], s2_send.at[k, j - 1],
                    s2_recv.at[k, j - 1], device(across(j) * 2 + core, me)))
        keep2[k] = set_sums(k, y)

    def cross_path(k):
        total = keep2[k]
        for j in range(1, n_y):
            copy(send2.at[k, j - 1], recv2.at[k, j - 1], s2_send.at[k, j - 1],
                 s2_recv.at[k, j - 1], device(partner, me)).wait_recv()
            total = total + recv2[k, j - 1].astype(F32)
        if k == 0:
            acc[...] = total
        else:
            send3[k - 1] = total.astype(BF16)
            go(copy(send3.at[k - 1], recv3.at[me], s3_send.at[k], s3_recv.at[me],
                    device(owner, order[k])))

    base_cols[...] = jnp.broadcast_to(base_ref[...], (cols, trades)).T
    for h in range(2):
        shift = jnp.where(core == h, 0, half)
        key = key_ref[...] - shift

        @pl.loop(0, n_y)
        def _(i):
            row = lax.broadcasted_iota(jnp.int32, (n_sets, trades), 0) + i * n_sets
            hot[h, pl.ds(pl.multiple_of(i * n_sets, n_sets), n_sets), :] = jnp.where(
                row == key, 1.0, 0.0
            ).astype(BF16)

    load.wait()

    for k in range(n_path + 2):
        if k + 1 < n_path:
            if k == 0:
                values(0)
                spread(1)
            relay(k + 1)
            if k + 2 < n_path:
                spread(k + 2)
        if 1 <= k < n_path:
            gathered(k)
            values(k)
        if 1 <= k < n_path + 1:
            cross_owner(k - 1)
        if k >= 2:
            cross_path(k - 2)

    floor = jnp.zeros((1, n_sets), F32)
    for a in range(posted_ref.shape[0]):
        floor = jnp.where(cset_ref[...] == a, posted_ref[a], floor)
    floor_cols = jnp.broadcast_to(floor, (cols, n_sets)).T
    lane_step = lax.broadcasted_iota(jnp.int32, (1, cols), 1) % steps
    factor = jnp.zeros((1, cols), F32)
    for s in range(steps):
        factor = jnp.where(lane_step == s, disc_ref[s], factor)
    nets = acc[...]
    for j in range(1, n_path):
        p = along(j)
        got = recv3.at[p]
        copy(got, got, s3_send.at[j], s3_recv.at[p], device(owner, p)).wait_recv()
        nets = nets + recv3[p].astype(F32)
    exposure = factor * jnp.maximum(nets - floor_cols, 0.0)
    exp_ref[...] = exposure

    pick = (
        lax.broadcasted_iota(jnp.int32, (8, cols), 1) % steps
        == lax.broadcasted_iota(jnp.int32, (8, cols), 0)
    ).astype(F32)
    tot[...] = lax.dot_general(
        pick, exposure, BY_LANES, precision=lax.Precision.HIGHEST, preferred_element_type=F32
    )
    for j in range(1, n_path):
        go(copy(tot, recv4.at[me], s4_send.at[j], s4_recv.at[me], device(owner, along(j))))
    sums = tot[...]
    for j in range(1, n_path):
        p = along(j)
        copy(tot, recv4.at[p], s4_send.at[j], s4_recv.at[p], device(owner, p)).wait_recv()
        sums = sums + recv4[p]
    mean_ref[...] = (sums / (cols // steps * n_path)).T[:, :steps]
    for c in open_sends:
        c.wait_send()


def shards(
    sensitivity,
    present_trade_value,
    trade_set_owner,
    trade_local_set,
    shocks,
    collateral_of_set,
    collateral_posted,
    discount,
):
    n_owner, n_path = lax.axis_size("owner"), lax.axis_size("path")
    trades, factors = sensitivity.shape
    steps = shocks.shape[1]
    cols = shocks.shape[0] * steps
    n_sets = collateral_of_set.shape[0]
    n_y = n_owner // 2
    half = n_y * n_sets
    owner_of = trade_set_owner[:, 0]
    key = (owner_of % 2) * half + (owner_of // 2) * n_sets + trade_local_set
    others = max(n_y - 1, 1)
    vmem = pl.BlockSpec(memory_space=pltpu.VMEM)
    smem = pl.BlockSpec(memory_space=pltpu.SMEM)
    dma = pltpu.SemaphoreType.DMA
    return pl.pallas_call(
        functools.partial(kernel, n_owner, n_path, n_sets, steps),
        out_shape=(
            jax.ShapeDtypeStruct((n_sets, cols), F32),
            jax.ShapeDtypeStruct((n_sets, steps), F32),
        ),
        in_specs=[pl.BlockSpec(memory_space=pl.ANY), vmem, vmem, vmem, vmem, smem, smem],
        out_specs=(vmem, vmem),
        scratch_shapes=[
            pltpu.VMEM((trades, factors), BF16),
            pltpu.VMEM((n_path, cols, factors), BF16),
            pltpu.VMEM((trades, cols), F32),
            pltpu.VMEM((2, half, trades), BF16),
            pltpu.VMEM((n_path, trades, cols), BF16),
            pltpu.VMEM((n_path, half, cols), F32),
            pltpu.VMEM((n_path, half, cols), F32),
            pltpu.VMEM((n_path, n_sets, cols), F32),
            pltpu.VMEM((n_path, others, n_sets, cols), BF16),
            pltpu.VMEM((n_path, others, n_sets, cols), BF16),
            pltpu.VMEM((n_sets, cols), F32),
            pltpu.VMEM((n_path - 1, n_sets, cols), BF16),
            pltpu.VMEM((n_path, n_sets, cols), BF16),
            pltpu.VMEM((8, n_sets), F32),
            pltpu.VMEM((n_path, 8, n_sets), F32),
            dma,
            dma((n_path,)), dma((n_path,)),
            dma((n_path, n_y)), dma((n_path, n_y)),
            dma((n_path, n_y)), dma((n_path, n_y)),
            dma((n_path,)), dma((n_path,)),
            dma((n_path, others)), dma((n_path, others)),
            dma((n_path,)), dma((n_path,)),
            dma((n_path,)), dma((n_path,)),
        ],
        compiler_params=pltpu.CompilerParams(
            collective_id=0, has_side_effects=True, vmem_limit_bytes=60 * 1024 * 1024
        ),
        cost_estimate=pl.CostEstimate(
            flops=2 * trades * cols * n_path * (factors + 2 * half),
            bytes_accessed=2 * trades * factors,
            transcendentals=0,
        ),
    )(
        sensitivity,
        shocks.reshape(cols, factors),
        present_trade_value.reshape(1, trades),
        key.reshape(1, trades),
        collateral_of_set.reshape(1, n_sets),
        collateral_posted,
        discount,
    )


def solution(mesh):
    in_specs = (
        P(("groups", "owner", "path"), None),
        P(("groups", "owner", "path")),
        P(("groups", "owner", "path"), None),
        P(("groups", "owner", "path")),
        P(("groups", "path"), None, None),
        P(("groups", "owner")),
        P("groups"),
        P("groups"),
    )
    out_specs = (P(("groups", "owner"), "path"), P(("groups", "owner"), None))
    return jax.shard_map(shards, mesh=mesh, in_specs=in_specs, out_specs=out_specs, check_vma=False)
```

```python
import functools

import jax
import jax.numpy as jnp
from jax import lax
from jax.experimental import pallas as pl
from jax.experimental.pallas import tpu as pltpu
from jax.sharding import PartitionSpec as P

MESH = pl.DeviceIdType.MESH
F32, BF16 = jnp.float32, jnp.bfloat16
BY_LANES = (((1,), (1,)), ((), ()))


def kernel(
    n_owner, n_path, n_sets, steps,
    sens_hbm, shock_ref, base_ref, owner_ref, local_ref, cset_ref, posted_ref, disc_ref,
    exp_ref, mean_ref,
    sens, moves, base_cols, hot, tv, send1, recv1, keep2, send2, recv2, acc, send3, recv3, tot, recv4,
    load_sem, a_send, a_recv, b_send, b_recv, c_send, c_recv,
    s1_send, s1_recv, s2_send, s2_recv, s3_send, s3_recv, s4_send, s4_recv,
):
    owner, me = lax.axis_index("owner"), lax.axis_index("path")
    n_y = n_owner // 2
    y, core = owner // 2, owner % 2
    partner = owner + 1 - 2 * core
    half = n_y * n_sets
    trades, factors = sens.shape
    cols = shock_ref.shape[0]
    piece = factors // n_owner
    open_sends, edge_sends = [], []

    def device(o, p):
        return {"owner": o, "path": p}

    def across(j):
        return lax.rem(y + j, n_y)

    def along(j):
        return lax.rem(me + j, n_path)

    load = pltpu.make_async_copy(sens_hbm, sens, load_sem)
    load.start()

    barrier = pltpu.get_barrier_semaphore()
    for j in range(1, n_path):
        pl.semaphore_signal(barrier, inc=1, device_id=device(owner, along(j)), device_id_type=MESH)
    for j in range(1, n_y):
        pl.semaphore_signal(
            barrier, inc=1, device_id=device(across(j) * 2 + core, me), device_id_type=MESH
        )
    pl.semaphore_signal(barrier, inc=1, device_id=device(partner, me), device_id_type=MESH)
    base_cols[...] = jnp.broadcast_to(base_ref[...], (cols, trades)).T
    pl.semaphore_wait(barrier, n_path - 1 + n_y - 1 + 1)

    low_side = me <= n_path - 1 - me
    both = jnp.where(low_side, me, n_path - 1 - me)
    order = []
    for k in range(n_path):
        swing = me - (k + 1) // 2 if k % 2 else me + k // 2
        order.append(jnp.where(k <= 2 * both, swing, jnp.where(low_side, k, n_path - 1 - k)))

    def lanes(o):
        return pl.ds(pl.multiple_of(o * piece, piece), piece)

    def copy(src, dst, send_sem, recv_sem, target):
        return pltpu.make_async_remote_copy(
            src_ref=src, dst_ref=dst, send_sem=send_sem, recv_sem=recv_sem,
            device_id=target, device_id_type=MESH,
        )

    def go(c):
        c.start()
        open_sends.append(c)

    def hop(src, target, slot, q):
        inside = (target >= 0) & (target < n_path)
        c = copy(src, moves.at[q, :, lanes(owner)], a_send.at[slot], a_recv.at[q],
                 device(owner, jnp.clip(target, 0, n_path - 1)))

        @pl.when(inside)
        def _():
            c.start()

        edge_sends.append((inside, c))

    hop(shock_ref.at[:, lanes(owner)], me + 1, 0, me)
    hop(shock_ref.at[:, lanes(owner)], me - 1, n_path, me)

    def spread(k):
        q = order[k]
        mine = moves.at[q, :, lanes(owner)]
        copy(mine, mine, a_send.at[k], a_recv.at[q], device(owner, q)).wait_recv()
        hop(mine, jnp.where(q < me, me + 1, me - 1), k, q)
        for j in range(1, n_y):
            go(copy(mine, mine, b_send.at[k, j], b_recv.at[q, j],
                    device(across(j) * 2 + core, me)))
        go(copy(mine, mine, c_send.at[k, 0], c_recv.at[q, 0], device(partner, me)))

    def relay(k):
        q = order[k]
        for j in range(1, n_y):
            source = across(n_y - j) * 2 + core
            got = moves.at[q, :, lanes(source)]
            copy(got, got, b_send.at[k, j], b_recv.at[q, j], device(partner, me)).wait_recv()
            go(copy(got, got, c_send.at[k, j], c_recv.at[q, j], device(partner, me)))

    def gathered(k):
        q = order[k]
        for j in range(n_y):
            got = moves.at[q, :, lanes(across(n_y - j) * 2 + 1 - core)]
            copy(got, got, c_send.at[k, j], c_recv.at[q, j], device(partner, me)).wait_recv()

    tile = min(trades, 512)

    def values(k):
        @pl.loop(0, trades // tile)
        def _(i):
            rows = pl.ds(pl.multiple_of(i * tile, tile), tile)
            block = shock_ref[...] if k == 0 else moves[order[k]]
            out = lax.dot_general(sens[rows, :], block, BY_LANES, preferred_element_type=F32)
            tv[k, rows, :] = (out + base_cols[rows, :]).astype(BF16)

        @pl.loop(0, n_y)
        def _(i):
            rows = pl.ds(pl.multiple_of(i * n_sets, n_sets), n_sets)
            send1[k, rows, :] = jnp.dot(hot[1, rows, :], tv[k], preferred_element_type=F32)

        go(copy(send1.at[k], recv1.at[k], s1_send.at[k], s1_recv.at[k], device(partner, me)))

    def set_sums(k, yy):
        rows = pl.ds(pl.multiple_of(yy * n_sets, n_sets), n_sets)
        return jnp.dot(hot[0, rows, :], tv[k], preferred_element_type=F32) + recv1[k, rows, :]

    def cross_owner(k):
        copy(send1.at[k], recv1.at[k], s1_send.at[k], s1_recv.at[k], device(partner, me)).wait_recv()
        for j in range(1, n_y):
            send2[k, j - 1] = set_sums(k, across(j)).astype(BF16)
            go(copy(send2.at[k, j - 1], recv2.at[k, j - 1], s2_send.at[k, j - 1],
                    s2_recv.at[k, j - 1], device(across(j) * 2 + core, me)))
        keep2[k] = set_sums(k, y)

    def cross_path(k):
        total = keep2[k]
        for j in range(1, n_y):
            copy(send2.at[k, j - 1], recv2.at[k, j - 1], s2_send.at[k, j - 1],
                 s2_recv.at[k, j - 1], device(partner, me)).wait_recv()
            total = total + recv2[k, j - 1].astype(F32)
        if k == 0:
            acc[...] = total
        else:
            send3[k - 1] = total.astype(BF16)
            go(copy(send3.at[k - 1], recv3.at[me], s3_send.at[k], s3_recv.at[me],
                    device(owner, order[k])))

    place = (owner_ref[...] % 2) * half + (owner_ref[...] // 2) * n_sets + local_ref[...]
    def one_hots(h):
        key = place - jnp.where(core == h, 0, half)

        @pl.loop(0, n_y)
        def _(i):
            row = lax.broadcasted_iota(jnp.int32, (n_sets, trades), 0) + i * n_sets
            hot[h, pl.ds(pl.multiple_of(i * n_sets, n_sets), n_sets), :] = jnp.where(
                row == key, 1.0, 0.0
            ).astype(BF16)

    one_hots(1)
    spread(1)
    one_hots(0)
    if n_path > 2:
        spread(2)
    load.wait()
    values(0)
    relay(1)
    for k in range(1, n_path + 2):
        if k + 2 < n_path:
            spread(k + 2)
        if k == 1 and n_path > 2:
            relay(2)
        if k < n_path:
            gathered(k)
            values(k)
        if 1 < k < n_path - 1:
            relay(k + 1)
        if k < n_path + 1:
            cross_owner(k - 1)
        if k >= 2:
            cross_path(k - 2)

    floor = jnp.zeros((1, n_sets), F32)
    for a in range(posted_ref.shape[0]):
        floor = jnp.where(cset_ref[...] == a, posted_ref[a], floor)
    floor_cols = jnp.broadcast_to(floor, (cols, n_sets)).T
    lane_step = lax.broadcasted_iota(jnp.int32, (1, cols), 1) % steps
    factor = jnp.zeros((1, cols), F32)
    for s in range(steps):
        factor = jnp.where(lane_step == s, disc_ref[s], factor)
    nets = acc[...]
    for j in range(1, n_path):
        p = along(j)
        got = recv3.at[p]
        copy(got, got, s3_send.at[j], s3_recv.at[p], device(owner, p)).wait_recv()
        nets = nets + recv3[p].astype(F32)
    exposure = factor * jnp.maximum(nets - floor_cols, 0.0)
    exp_ref[...] = exposure

    pick = (
        lax.broadcasted_iota(jnp.int32, (8, cols), 1) % steps
        == lax.broadcasted_iota(jnp.int32, (8, cols), 0)
    ).astype(F32)
    tot[...] = lax.dot_general(
        pick, exposure, BY_LANES, precision=lax.Precision.HIGHEST, preferred_element_type=F32
    )
    for j in range(1, n_path):
        go(copy(tot, recv4.at[me], s4_send.at[j], s4_recv.at[me], device(owner, along(j))))
    sums = tot[...]
    for j in range(1, n_path):
        p = along(j)
        copy(tot, recv4.at[p], s4_send.at[j], s4_recv.at[p], device(owner, p)).wait_recv()
        sums = sums + recv4[p]
    mean_ref[...] = (sums / (cols // steps * n_path))[:steps, :]
    for c in open_sends:
        c.wait_send()
    for inside, c in edge_sends:

        @pl.when(inside)
        def _():
            c.wait_send()


def shards(
    sensitivity,
    present_trade_value,
    trade_set_owner,
    trade_local_set,
    shocks,
    collateral_of_set,
    collateral_posted,
    discount,
):
    n_owner, n_path = lax.axis_size("owner"), lax.axis_size("path")
    trades, factors = sensitivity.shape
    steps = shocks.shape[1]
    cols = shocks.shape[0] * steps
    n_sets = collateral_of_set.shape[0]
    n_y = n_owner // 2
    half = n_y * n_sets
    others = max(n_y - 1, 1)
    vmem = pl.BlockSpec(memory_space=pltpu.VMEM)
    smem = pl.BlockSpec(memory_space=pltpu.SMEM)
    dma = pltpu.SemaphoreType.DMA
    exposure, mean = pl.pallas_call(
        functools.partial(kernel, n_owner, n_path, n_sets, steps),
        out_shape=(
            jax.ShapeDtypeStruct((n_sets, cols), F32),
            jax.ShapeDtypeStruct((steps, n_sets), F32),
        ),
        in_specs=[pl.BlockSpec(memory_space=pl.ANY), vmem, vmem, vmem, vmem, vmem, smem, smem],
        out_specs=(vmem, vmem),
        scratch_shapes=[
            pltpu.VMEM((trades, factors), BF16),
            pltpu.VMEM((n_path, cols, factors), BF16),
            pltpu.VMEM((trades, cols), F32),
            pltpu.VMEM((2, half, trades), BF16),
            pltpu.VMEM((n_path, trades, cols), BF16),
            pltpu.VMEM((n_path, half, cols), F32),
            pltpu.VMEM((n_path, half, cols), F32),
            pltpu.VMEM((n_path, n_sets, cols), F32),
            pltpu.VMEM((n_path, others, n_sets, cols), BF16),
            pltpu.VMEM((n_path, others, n_sets, cols), BF16),
            pltpu.VMEM((n_sets, cols), F32),
            pltpu.VMEM((n_path - 1, n_sets, cols), BF16),
            pltpu.VMEM((n_path, n_sets, cols), BF16),
            pltpu.VMEM((8, n_sets), F32),
            pltpu.VMEM((n_path, 8, n_sets), F32),
            dma,
            dma((n_path + 1,)), dma((n_path,)),
            dma((n_path, n_y)), dma((n_path, n_y)),
            dma((n_path, n_y)), dma((n_path, n_y)),
            dma((n_path,)), dma((n_path,)),
            dma((n_path, others)), dma((n_path, others)),
            dma((n_path,)), dma((n_path,)),
            dma((n_path,)), dma((n_path,)),
        ],
        compiler_params=pltpu.CompilerParams(
            collective_id=0, has_side_effects=True, vmem_limit_bytes=60 * 1024 * 1024
        ),
        cost_estimate=pl.CostEstimate(
            flops=2 * trades * cols * n_path * (factors + 2 * half),
            bytes_accessed=2 * trades * factors,
            transcendentals=0,
        ),
    )(
        sensitivity,
        shocks.reshape(cols, factors),
        present_trade_value.reshape(1, trades),
        trade_set_owner.reshape(1, trades),
        trade_local_set.reshape(1, trades),
        collateral_of_set.reshape(1, n_sets),
        collateral_posted,
        discount,
    )
    return exposure, mean.T


def solution(mesh):
    in_specs = (
        P(("groups", "owner", "path"), None),
        P(("groups", "owner", "path")),
        P(("groups", "owner", "path"), None),
        P(("groups", "owner", "path")),
        P(("groups", "path"), None, None),
        P(("groups", "owner")),
        P("groups"),
        P("groups"),
    )
    out_specs = (P(("groups", "owner"), "path"), P(("groups", "owner"), None))
    return jax.shard_map(shards, mesh=mesh, in_specs=in_specs, out_specs=out_specs, check_vma=False)
```

```python
import functools

import jax
import jax.numpy as jnp
from jax import lax
from jax.experimental import pallas as pl
from jax.experimental.pallas import tpu as pltpu
from jax.sharding import PartitionSpec as P

MESH = pl.DeviceIdType.MESH
F32, BF16 = jnp.float32, jnp.bfloat16
PARTS = 2
BY_LANES = (((1,), (1,)), ((), ()))


def kernel(
    n_owner, n_path, n_sets, steps,
    sens_hbm, shock_block, base_ref, owner_ref, local_ref, cset_ref, posted_ref, disc_ref,
    exp_ref, mean_ref,
    shock_ref, sens, moves, base_cols, hot, tv, send1, recv1, keep2, send2, recv2, acc, send3, recv3, tot, recv4,
    load_sem, a_send, a_recv, b_send, b_recv, c_send, c_recv,
    s1_send, s1_recv, s2_send, s2_recv, s3_send, s3_recv, s4_send, s4_recv,
):
    owner, me = lax.axis_index("owner"), lax.axis_index("path")
    n_y = n_owner // 2
    y, core = owner // 2, owner % 2
    partner = owner + 1 - 2 * core
    half = n_y * n_sets
    trades, factors = sens.shape
    cols = shock_ref.shape[0]
    piece = factors // n_owner
    open_sends, edge_sends = [], []

    def device(o, p):
        return {"owner": o, "path": p}

    def across(j):
        return lax.rem(y + j, n_y)

    def along(j):
        return lax.rem(me + j, n_path)

    load = pltpu.make_async_copy(sens_hbm, sens, load_sem)
    load.start()

    barrier = pltpu.get_barrier_semaphore()
    for j in range(1, n_path):
        pl.semaphore_signal(barrier, inc=1, device_id=device(owner, along(j)), device_id_type=MESH)
    for j in range(1, n_y):
        pl.semaphore_signal(
            barrier, inc=1, device_id=device(across(j) * 2 + core, me), device_id_type=MESH
        )
    pl.semaphore_signal(barrier, inc=1, device_id=device(partner, me), device_id_type=MESH)
    shock_ref[...] = shock_block[...].reshape(cols, factors)
    base_cols[...] = jnp.broadcast_to(base_ref[...], (cols, trades)).T
    pl.semaphore_wait(barrier, n_path - 1 + n_y - 1 + 1)

    low_side = me <= n_path - 1 - me
    both = jnp.where(low_side, me, n_path - 1 - me)
    order = []
    for k in range(n_path):
        swing = me - (k + 1) // 2 if k % 2 else me + k // 2
        order.append(jnp.where(k <= 2 * both, swing, jnp.where(low_side, k, n_path - 1 - k)))

    def lanes(o):
        return pl.ds(pl.multiple_of(o * piece, piece), piece)

    def copy(src, dst, send_sem, recv_sem, target):
        return pltpu.make_async_remote_copy(
            src_ref=src, dst_ref=dst, send_sem=send_sem, recv_sem=recv_sem,
            device_id=target, device_id_type=MESH,
        )

    def go(c):
        c.start()
        open_sends.append(c)

    def rows_of(part):
        return pl.ds(part * (cols // PARTS), cols // PARTS)

    def hop(src, target, slot, q, part):
        inside = (target >= 0) & (target < n_path)
        c = copy(src, moves.at[q, rows_of(part), lanes(owner)], a_send.at[slot, part],
                 a_recv.at[q, part], device(owner, jnp.clip(target, 0, n_path - 1)))

        @pl.when(inside)
        def _():
            c.start()

        edge_sends.append((inside, c))

    for part in range(PARTS):
        hop(shock_ref.at[rows_of(part), lanes(owner)], me + 1, 0, me, part)
        hop(shock_ref.at[rows_of(part), lanes(owner)], me - 1, n_path, me, part)

    def spread(k):
        q = order[k]
        for part in range(PARTS):
            mine = moves.at[q, rows_of(part), lanes(owner)]
            copy(mine, mine, a_send.at[k, part], a_recv.at[q, part], device(owner, q)).wait_recv()
            hop(mine, jnp.where(q < me, me + 1, me - 1), k, q, part)
            for j in range(1, n_y):
                go(copy(mine, mine, b_send.at[k, j, part], b_recv.at[q, j, part],
                        device(across(j) * 2 + core, me)))
            go(copy(mine, mine, c_send.at[k, 0, part], c_recv.at[q, 0, part], device(partner, me)))

    def relay(k):
        q = order[k]
        for part in range(PARTS):
            for j in range(1, n_y):
                source = across(n_y - j) * 2 + core
                got = moves.at[q, rows_of(part), lanes(source)]
                copy(got, got, b_send.at[k, j, part], b_recv.at[q, j, part],
                     device(partner, me)).wait_recv()
                go(copy(got, got, c_send.at[k, j, part], c_recv.at[q, j, part],
                        device(partner, me)))

    def gathered(k):
        q = order[k]
        for part in range(PARTS):
            for j in range(n_y):
                got = moves.at[q, rows_of(part), lanes(across(n_y - j) * 2 + 1 - core)]
                copy(got, got, c_send.at[k, j, part], c_recv.at[q, j, part],
                     device(partner, me)).wait_recv()

    tile = min(trades, 512)

    def values(k):
        @pl.loop(0, trades // tile)
        def _(i):
            rows = pl.ds(pl.multiple_of(i * tile, tile), tile)
            block = shock_ref[...] if k == 0 else moves[order[k]]
            out = lax.dot_general(sens[rows, :], block, BY_LANES, preferred_element_type=F32)
            tv[k, rows, :] = (out + base_cols[rows, :]).astype(BF16)

        @pl.loop(0, n_y)
        def _(i):
            rows = pl.ds(pl.multiple_of(i * n_sets, n_sets), n_sets)
            send1[k, rows, :] = jnp.dot(hot[1, rows, :], tv[k], preferred_element_type=F32)

        go(copy(send1.at[k], recv1.at[k], s1_send.at[k], s1_recv.at[k], device(partner, me)))

    def set_sums(k, yy):
        rows = pl.ds(pl.multiple_of(yy * n_sets, n_sets), n_sets)
        return jnp.dot(hot[0, rows, :], tv[k], preferred_element_type=F32) + recv1[k, rows, :]

    def cross_owner(k):
        copy(send1.at[k], recv1.at[k], s1_send.at[k], s1_recv.at[k], device(partner, me)).wait_recv()
        for j in range(1, n_y):
            send2[k, j - 1] = set_sums(k, across(j)).astype(BF16)
            go(copy(send2.at[k, j - 1], recv2.at[k, j - 1], s2_send.at[k, j - 1],
                    s2_recv.at[k, j - 1], device(across(j) * 2 + core, me)))
        keep2[k] = set_sums(k, y)

    def cross_path(k):
        total = keep2[k]
        for j in range(1, n_y):
            copy(send2.at[k, j - 1], recv2.at[k, j - 1], s2_send.at[k, j - 1],
                 s2_recv.at[k, j - 1], device(partner, me)).wait_recv()
            total = total + recv2[k, j - 1].astype(F32)
        if k == 0:
            acc[...] = total
        else:
            send3[k - 1] = total.astype(BF16)
            go(copy(send3.at[k - 1], recv3.at[me], s3_send.at[k], s3_recv.at[me],
                    device(owner, order[k])))

    place = (owner_ref[...] % 2) * half + (owner_ref[...] // 2) * n_sets + local_ref[...]
    def one_hots(h):
        key = place - jnp.where(core == h, 0, half)

        @pl.loop(0, n_y)
        def _(i):
            row = lax.broadcasted_iota(jnp.int32, (n_sets, trades), 0) + i * n_sets
            hot[h, pl.ds(pl.multiple_of(i * n_sets, n_sets), n_sets), :] = jnp.where(
                row == key, 1.0, 0.0
            ).astype(BF16)

    one_hots(1)
    spread(1)
    one_hots(0)
    if n_path > 2:
        spread(2)
    load.wait()
    values(0)
    relay(1)
    for k in range(1, n_path + 2):
        if k + 2 < n_path:
            spread(k + 2)
        if k == 1 and n_path > 2:
            relay(2)
        if k < n_path:
            gathered(k)
            values(k)
        if 1 < k < n_path - 1:
            relay(k + 1)
        if k < n_path + 1:
            cross_owner(k - 1)
        if k >= 2:
            cross_path(k - 2)

    floor = jnp.zeros((1, n_sets), F32)
    for a in range(posted_ref.shape[0]):
        floor = jnp.where(cset_ref[...] == a, posted_ref[a], floor)
    floor_cols = jnp.broadcast_to(floor, (cols, n_sets)).T
    lane_step = lax.broadcasted_iota(jnp.int32, (1, cols), 1) % steps
    factor = jnp.zeros((1, cols), F32)
    for s in range(steps):
        factor = jnp.where(lane_step == s, disc_ref[s], factor)
    nets = acc[...]
    for j in range(1, n_path):
        p = along(j)
        got = recv3.at[p]
        copy(got, got, s3_send.at[j], s3_recv.at[p], device(owner, p)).wait_recv()
        nets = nets + recv3[p].astype(F32)
    exposure = factor * jnp.maximum(nets - floor_cols, 0.0)
    exp_ref[...] = exposure

    pick = (
        lax.broadcasted_iota(jnp.int32, (8, cols), 1) % steps
        == lax.broadcasted_iota(jnp.int32, (8, cols), 0)
    ).astype(F32)
    tot[...] = lax.dot_general(
        pick, exposure, BY_LANES, precision=lax.Precision.HIGHEST, preferred_element_type=F32
    )
    for j in range(1, n_path):
        go(copy(tot, recv4.at[me], s4_send.at[j], s4_recv.at[me], device(owner, along(j))))
    sums = tot[...]
    for j in range(1, n_path):
        p = along(j)
        copy(tot, recv4.at[p], s4_send.at[j], s4_recv.at[p], device(owner, p)).wait_recv()
        sums = sums + recv4[p]
    mean_ref[...] = (sums / (cols // steps * n_path))[:steps, :]
    for c in open_sends:
        c.wait_send()
    for inside, c in edge_sends:

        @pl.when(inside)
        def _():
            c.wait_send()


def shards(
    sensitivity,
    present_trade_value,
    trade_set_owner,
    trade_local_set,
    shocks,
    collateral_of_set,
    collateral_posted,
    discount,
):
    n_owner, n_path = lax.axis_size("owner"), lax.axis_size("path")
    trades, factors = sensitivity.shape
    steps = shocks.shape[1]
    cols = shocks.shape[0] * steps
    n_sets = collateral_of_set.shape[0]
    n_y = n_owner // 2
    half = n_y * n_sets
    others = max(n_y - 1, 1)
    vmem = pl.BlockSpec(memory_space=pltpu.VMEM)
    smem = pl.BlockSpec(memory_space=pltpu.SMEM)
    dma = pltpu.SemaphoreType.DMA
    exposure, mean = pl.pallas_call(
        functools.partial(kernel, n_owner, n_path, n_sets, steps),
        out_shape=(
            jax.ShapeDtypeStruct((n_sets, cols), F32),
            jax.ShapeDtypeStruct((steps, n_sets), F32),
        ),
        in_specs=[pl.BlockSpec(memory_space=pl.ANY), vmem, vmem, vmem, vmem, vmem, smem, smem],
        out_specs=(vmem, vmem),
        scratch_shapes=[
            pltpu.VMEM((cols, factors), BF16),
            pltpu.VMEM((trades, factors), BF16),
            pltpu.VMEM((n_path, cols, factors), BF16),
            pltpu.VMEM((trades, cols), F32),
            pltpu.VMEM((2, half, trades), BF16),
            pltpu.VMEM((n_path, trades, cols), BF16),
            pltpu.VMEM((n_path, half, cols), F32),
            pltpu.VMEM((n_path, half, cols), F32),
            pltpu.VMEM((n_path, n_sets, cols), F32),
            pltpu.VMEM((n_path, others, n_sets, cols), BF16),
            pltpu.VMEM((n_path, others, n_sets, cols), BF16),
            pltpu.VMEM((n_sets, cols), F32),
            pltpu.VMEM((n_path - 1, n_sets, cols), BF16),
            pltpu.VMEM((n_path, n_sets, cols), BF16),
            pltpu.VMEM((8, n_sets), F32),
            pltpu.VMEM((n_path, 8, n_sets), F32),
            dma,
            dma((n_path + 1, PARTS)), dma((n_path, PARTS)),
            dma((n_path, n_y, PARTS)), dma((n_path, n_y, PARTS)),
            dma((n_path, n_y, PARTS)), dma((n_path, n_y, PARTS)),
            dma((n_path,)), dma((n_path,)),
            dma((n_path, others)), dma((n_path, others)),
            dma((n_path,)), dma((n_path,)),
            dma((n_path,)), dma((n_path,)),
        ],
        compiler_params=pltpu.CompilerParams(
            collective_id=0, has_side_effects=True, vmem_limit_bytes=60 * 1024 * 1024
        ),
        cost_estimate=pl.CostEstimate(
            flops=2 * trades * cols * n_path * (factors + 2 * half),
            bytes_accessed=2 * trades * factors,
            transcendentals=0,
        ),
    )(
        sensitivity,
        shocks,
        present_trade_value.reshape(1, trades),
        trade_set_owner.reshape(1, trades),
        trade_local_set.reshape(1, trades),
        collateral_of_set.reshape(1, n_sets),
        collateral_posted,
        discount,
    )
    return exposure, mean.T


def solution(mesh):
    in_specs = (
        P(("groups", "owner", "path"), None),
        P(("groups", "owner", "path")),
        P(("groups", "owner", "path"), None),
        P(("groups", "owner", "path")),
        P(("groups", "path"), None, None),
        P(("groups", "owner")),
        P("groups"),
        P("groups"),
    )
    out_specs = (P(("groups", "owner"), "path"), P(("groups", "owner"), None))
    return jax.shard_map(shards, mesh=mesh, in_specs=in_specs, out_specs=out_specs, check_vma=False)
```

```python
import functools

import jax
import jax.numpy as jnp
from jax import lax
from jax.experimental import pallas as pl
from jax.experimental.pallas import tpu as pltpu
from jax.sharding import PartitionSpec as P

MESH = pl.DeviceIdType.MESH
F32, BF16 = jnp.float32, jnp.bfloat16
PARTS = 2
BY_LANES = (((1,), (1,)), ((), ()))


def kernel(
    n_owner, n_path, n_sets, steps,
    sens_hbm, shock_block, base_ref, owner_ref, local_ref, cset_ref, posted_ref, disc_ref,
    exp_ref, mean_ref,
    shock_ref, sens, moves, base_cols, hot, tv, send1, recv1, keep2, send2, recv2, acc, send3, recv3, tot, recv4,
    load_sem, a_send, a_recv, b_send, b_recv, c_send, c_recv,
    s1_send, s1_recv, s2_send, s2_recv, s3_send, s3_recv, s4_send, s4_recv,
):
    owner, me = lax.axis_index("owner"), lax.axis_index("path")
    n_y = n_owner // 2
    y, core = owner // 2, owner % 2
    partner = owner + 1 - 2 * core
    half = n_y * n_sets
    trades, factors = sens.shape
    cols = shock_ref.shape[0]
    piece = factors // n_owner
    open_sends, edge_sends = [], []

    def device(o, p):
        return {"owner": o, "path": p}

    def across(j):
        return lax.rem(y + j, n_y)

    def along(j):
        return lax.rem(me + j, n_path)

    load = pltpu.make_async_copy(sens_hbm, sens, load_sem)
    load.start()

    barrier = pltpu.get_barrier_semaphore()
    for j in range(1, n_path):
        pl.semaphore_signal(barrier, inc=1, device_id=device(owner, along(j)), device_id_type=MESH)
    for j in range(1, n_y):
        pl.semaphore_signal(
            barrier, inc=1, device_id=device(across(j) * 2 + core, me), device_id_type=MESH
        )
    pl.semaphore_signal(barrier, inc=1, device_id=device(partner, me), device_id_type=MESH)
    shock_ref[...] = shock_block[...].reshape(cols, factors)
    base_cols[...] = jnp.broadcast_to(base_ref[...], (cols, trades)).T
    pl.semaphore_wait(barrier, n_path - 1 + n_y - 1 + 1)

    low_side = me <= n_path - 1 - me
    both = jnp.where(low_side, me, n_path - 1 - me)
    order = []
    for k in range(n_path):
        swing = me - (k + 1) // 2 if k % 2 else me + k // 2
        order.append(jnp.where(k <= 2 * both, swing, jnp.where(low_side, k, n_path - 1 - k)))

    def lanes(o):
        return pl.ds(pl.multiple_of(o * piece, piece), piece)

    def copy(src, dst, send_sem, recv_sem, target):
        return pltpu.make_async_remote_copy(
            src_ref=src, dst_ref=dst, send_sem=send_sem, recv_sem=recv_sem,
            device_id=target, device_id_type=MESH,
        )

    def go(c):
        c.start()
        open_sends.append(c)

    def rows_of(part):
        return pl.ds(part * (cols // PARTS), cols // PARTS)

    def hop(src, target, slot, q, part):
        inside = (target >= 0) & (target < n_path)
        c = copy(src, moves.at[q, rows_of(part), lanes(owner)], a_send.at[slot, part],
                 a_recv.at[q, part], device(owner, jnp.clip(target, 0, n_path - 1)))

        @pl.when(inside)
        def _():
            c.start()

        edge_sends.append((inside, c))

    for part in range(PARTS):
        hop(shock_ref.at[rows_of(part), lanes(owner)], me + 1, 0, me, part)
        hop(shock_ref.at[rows_of(part), lanes(owner)], me - 1, n_path, me, part)

    def spread(k):
        q = order[k]
        for part in range(PARTS):
            mine = moves.at[q, rows_of(part), lanes(owner)]
            copy(mine, mine, a_send.at[k, part], a_recv.at[q, part], device(owner, q)).wait_recv()
            hop(mine, jnp.where(q < me, me + 1, me - 1), k, q, part)
            for j in range(1, n_y):
                go(copy(mine, mine, b_send.at[k, j, part], b_recv.at[q, j, part],
                        device(across(j) * 2 + core, me)))
            go(copy(mine, mine, c_send.at[k, 0, part], c_recv.at[q, 0, part], device(partner, me)))

    def relay(k):
        q = order[k]
        for part in range(PARTS):
            for j in range(1, n_y):
                source = across(n_y - j) * 2 + core
                got = moves.at[q, rows_of(part), lanes(source)]
                copy(got, got, b_send.at[k, j, part], b_recv.at[q, j, part],
                     device(partner, me)).wait_recv()
                go(copy(got, got, c_send.at[k, j, part], c_recv.at[q, j, part],
                        device(partner, me)))

    def gathered(k):
        q = order[k]
        for part in range(PARTS):
            for j in range(n_y):
                got = moves.at[q, rows_of(part), lanes(across(n_y - j) * 2 + 1 - core)]
                copy(got, got, c_send.at[k, j, part], c_recv.at[q, j, part],
                     device(partner, me)).wait_recv()

    tile = min(trades, 512)

    def values(k):
        @pl.loop(0, trades // tile)
        def _(i):
            rows = pl.ds(pl.multiple_of(i * tile, tile), tile)
            block = shock_ref[...] if k == 0 else moves[order[k]]
            out = lax.dot_general(sens[rows, :], block, BY_LANES, preferred_element_type=F32)
            tv[k, rows, :] = (out + base_cols[rows, :]).astype(BF16)

        @pl.loop(0, n_y)
        def _(i):
            rows = pl.ds(pl.multiple_of(i * n_sets, n_sets), n_sets)
            part_sums = jnp.dot(hot[1, rows, :], tv[k], preferred_element_type=F32)
            send1[k, rows, :] = part_sums.astype(BF16)

        go(copy(send1.at[k], recv1.at[k], s1_send.at[k], s1_recv.at[k], device(partner, me)))

    def set_sums(k, yy):
        rows = pl.ds(pl.multiple_of(yy * n_sets, n_sets), n_sets)
        return jnp.dot(hot[0, rows, :], tv[k], preferred_element_type=F32) + recv1[k, rows, :].astype(F32)

    def cross_owner(k):
        copy(send1.at[k], recv1.at[k], s1_send.at[k], s1_recv.at[k], device(partner, me)).wait_recv()
        for j in range(1, n_y):
            send2[k, j - 1] = set_sums(k, across(j)).astype(BF16)
            go(copy(send2.at[k, j - 1], recv2.at[k, j - 1], s2_send.at[k, j - 1],
                    s2_recv.at[k, j - 1], device(across(j) * 2 + core, me)))
        keep2[k] = set_sums(k, y)

    def cross_path(k):
        total = keep2[k]
        for j in range(1, n_y):
            copy(send2.at[k, j - 1], recv2.at[k, j - 1], s2_send.at[k, j - 1],
                 s2_recv.at[k, j - 1], device(partner, me)).wait_recv()
            total = total + recv2[k, j - 1].astype(F32)
        if k == 0:
            acc[...] = total
        else:
            send3[k - 1] = total.astype(BF16)
            go(copy(send3.at[k - 1], recv3.at[me], s3_send.at[k], s3_recv.at[me],
                    device(owner, order[k])))

    place = (owner_ref[...] % 2) * half + (owner_ref[...] // 2) * n_sets + local_ref[...]
    def one_hots(h):
        key = place - jnp.where(core == h, 0, half)

        @pl.loop(0, n_y)
        def _(i):
            row = lax.broadcasted_iota(jnp.int32, (n_sets, trades), 0) + i * n_sets
            hot[h, pl.ds(pl.multiple_of(i * n_sets, n_sets), n_sets), :] = jnp.where(
                row == key, 1.0, 0.0
            ).astype(BF16)

    one_hots(1)
    spread(1)
    one_hots(0)
    if n_path > 2:
        spread(2)
    load.wait()
    values(0)
    relay(1)
    for k in range(1, n_path + 2):
        if k + 2 < n_path:
            spread(k + 2)
        if k == 1 and n_path > 2:
            relay(2)
        if k < n_path:
            gathered(k)
            values(k)
        if 1 < k < n_path - 1:
            relay(k + 1)
        if k < n_path + 1:
            cross_owner(k - 1)
        if k >= 2:
            cross_path(k - 2)

    floor = jnp.zeros((1, n_sets), F32)
    for a in range(posted_ref.shape[0]):
        floor = jnp.where(cset_ref[...] == a, posted_ref[a], floor)
    floor_cols = jnp.broadcast_to(floor, (cols, n_sets)).T
    lane_step = lax.broadcasted_iota(jnp.int32, (1, cols), 1) % steps
    factor = jnp.zeros((1, cols), F32)
    for s in range(steps):
        factor = jnp.where(lane_step == s, disc_ref[s], factor)
    nets = acc[...]
    for j in range(1, n_path):
        p = along(j)
        got = recv3.at[p]
        copy(got, got, s3_send.at[j], s3_recv.at[p], device(owner, p)).wait_recv()
        nets = nets + recv3[p].astype(F32)
    exposure = factor * jnp.maximum(nets - floor_cols, 0.0)
    exp_ref[...] = exposure

    pick = (
        lax.broadcasted_iota(jnp.int32, (8, cols), 1) % steps
        == lax.broadcasted_iota(jnp.int32, (8, cols), 0)
    ).astype(F32)
    tot[...] = lax.dot_general(
        pick, exposure, BY_LANES, precision=lax.Precision.HIGHEST, preferred_element_type=F32
    )
    for j in range(1, n_path):
        go(copy(tot, recv4.at[me], s4_send.at[j], s4_recv.at[me], device(owner, along(j))))
    sums = tot[...]
    for j in range(1, n_path):
        p = along(j)
        copy(tot, recv4.at[p], s4_send.at[j], s4_recv.at[p], device(owner, p)).wait_recv()
        sums = sums + recv4[p]
    mean_ref[...] = (sums / (cols // steps * n_path))[:steps, :]
    for c in open_sends:
        c.wait_send()
    for inside, c in edge_sends:

        @pl.when(inside)
        def _():
            c.wait_send()


def shards(
    sensitivity,
    present_trade_value,
    trade_set_owner,
    trade_local_set,
    shocks,
    collateral_of_set,
    collateral_posted,
    discount,
):
    n_owner, n_path = lax.axis_size("owner"), lax.axis_size("path")
    trades, factors = sensitivity.shape
    steps = shocks.shape[1]
    cols = shocks.shape[0] * steps
    n_sets = collateral_of_set.shape[0]
    n_y = n_owner // 2
    half = n_y * n_sets
    others = max(n_y - 1, 1)
    vmem = pl.BlockSpec(memory_space=pltpu.VMEM)
    smem = pl.BlockSpec(memory_space=pltpu.SMEM)
    dma = pltpu.SemaphoreType.DMA
    exposure, mean = pl.pallas_call(
        functools.partial(kernel, n_owner, n_path, n_sets, steps),
        out_shape=(
            jax.ShapeDtypeStruct((n_sets, cols), F32),
            jax.ShapeDtypeStruct((steps, n_sets), F32),
        ),
        in_specs=[pl.BlockSpec(memory_space=pl.ANY), vmem, vmem, vmem, vmem, vmem, smem, smem],
        out_specs=(vmem, vmem),
        scratch_shapes=[
            pltpu.VMEM((cols, factors), BF16),
            pltpu.VMEM((trades, factors), BF16),
            pltpu.VMEM((n_path, cols, factors), BF16),
            pltpu.VMEM((trades, cols), F32),
            pltpu.VMEM((2, half, trades), BF16),
            pltpu.VMEM((n_path, trades, cols), BF16),
            pltpu.VMEM((n_path, half, cols), BF16),
            pltpu.VMEM((n_path, half, cols), BF16),
            pltpu.VMEM((n_path, n_sets, cols), F32),
            pltpu.VMEM((n_path, others, n_sets, cols), BF16),
            pltpu.VMEM((n_path, others, n_sets, cols), BF16),
            pltpu.VMEM((n_sets, cols), F32),
            pltpu.VMEM((n_path - 1, n_sets, cols), BF16),
            pltpu.VMEM((n_path, n_sets, cols), BF16),
            pltpu.VMEM((8, n_sets), F32),
            pltpu.VMEM((n_path, 8, n_sets), F32),
            dma,
            dma((n_path + 1, PARTS)), dma((n_path, PARTS)),
            dma((n_path, n_y, PARTS)), dma((n_path, n_y, PARTS)),
            dma((n_path, n_y, PARTS)), dma((n_path, n_y, PARTS)),
            dma((n_path,)), dma((n_path,)),
            dma((n_path, others)), dma((n_path, others)),
            dma((n_path,)), dma((n_path,)),
            dma((n_path,)), dma((n_path,)),
        ],
        compiler_params=pltpu.CompilerParams(
            collective_id=0, has_side_effects=True, vmem_limit_bytes=60 * 1024 * 1024
        ),
        cost_estimate=pl.CostEstimate(
            flops=2 * trades * cols * n_path * (factors + 2 * half),
            bytes_accessed=2 * trades * factors,
            transcendentals=0,
        ),
    )(
        sensitivity,
        shocks,
        present_trade_value.reshape(1, trades),
        trade_set_owner.reshape(1, trades),
        trade_local_set.reshape(1, trades),
        collateral_of_set.reshape(1, n_sets),
        collateral_posted,
        discount,
    )
    return exposure, mean.T


def solution(mesh):
    in_specs = (
        P(("groups", "owner", "path"), None),
        P(("groups", "owner", "path")),
        P(("groups", "owner", "path"), None),
        P(("groups", "owner", "path")),
        P(("groups", "path"), None, None),
        P(("groups", "owner")),
        P("groups"),
        P("groups"),
    )
    out_specs = (P(("groups", "owner"), "path"), P(("groups", "owner"), None))
    return jax.shard_map(shards, mesh=mesh, in_specs=in_specs, out_specs=out_specs, check_vma=False)
```

```python
import functools

import jax
import jax.numpy as jnp
from jax import lax
from jax.experimental import pallas as pl
from jax.experimental.pallas import tpu as pltpu
from jax.sharding import PartitionSpec as P

MESH = pl.DeviceIdType.MESH
F32, BF16 = jnp.float32, jnp.bfloat16
PARTS = 2
BY_LANES = (((1,), (1,)), ((), ()))


def kernel(
    n_owner, n_path, n_sets, steps,
    sens_hbm, shock_block, base_ref, owner_ref, local_ref, cset_ref, posted_ref, disc_ref,
    exp_ref, mean_ref,
    shock_ref, sens, moves, base_cols, floor_cols, hot, tv, send1, recv1, keep2, send2, recv2, acc, send3, recv3, tot, recv4,
    load_sem, a_send, a_recv, b_send, b_recv, c_send, c_recv,
    s1_send, s1_recv, s2_send, s2_recv, s3_send, s3_recv, s4_send, s4_recv,
):
    owner, me = lax.axis_index("owner"), lax.axis_index("path")
    n_y = n_owner // 2
    y, core = owner // 2, owner % 2
    partner = owner + 1 - 2 * core
    half = n_y * n_sets
    trades, factors = sens.shape
    cols = shock_ref.shape[0]
    piece = factors // n_owner
    open_sends, edge_sends = [], []

    def device(o, p):
        return {"owner": o, "path": p}

    def across(j):
        return lax.rem(y + j, n_y)

    def along(j):
        return lax.rem(me + j, n_path)

    load = pltpu.make_async_copy(sens_hbm, sens, load_sem)
    load.start()

    barrier = pltpu.get_barrier_semaphore()
    for j in range(1, n_path):
        pl.semaphore_signal(barrier, inc=1, device_id=device(owner, along(j)), device_id_type=MESH)
    for j in range(1, n_y):
        pl.semaphore_signal(
            barrier, inc=1, device_id=device(across(j) * 2 + core, me), device_id_type=MESH
        )
    pl.semaphore_signal(barrier, inc=1, device_id=device(partner, me), device_id_type=MESH)
    shock_ref[...] = shock_block[...].reshape(cols, factors)
    pl.semaphore_wait(barrier, n_path - 1 + n_y - 1 + 1)

    low_side = me <= n_path - 1 - me
    both = jnp.where(low_side, me, n_path - 1 - me)
    order = []
    for k in range(n_path):
        swing = me - (k + 1) // 2 if k % 2 else me + k // 2
        order.append(jnp.where(k <= 2 * both, swing, jnp.where(low_side, k, n_path - 1 - k)))

    def lanes(o):
        return pl.ds(pl.multiple_of(o * piece, piece), piece)

    def copy(src, dst, send_sem, recv_sem, target):
        return pltpu.make_async_remote_copy(
            src_ref=src, dst_ref=dst, send_sem=send_sem, recv_sem=recv_sem,
            device_id=target, device_id_type=MESH,
        )

    def go(c):
        c.start()
        open_sends.append(c)

    def rows_of(part):
        return pl.ds(part * (cols // PARTS), cols // PARTS)

    def hop(src, target, slot, q, part):
        inside = (target >= 0) & (target < n_path)
        c = copy(src, moves.at[q, rows_of(part), lanes(owner)], a_send.at[slot, part],
                 a_recv.at[q, part], device(owner, jnp.clip(target, 0, n_path - 1)))

        @pl.when(inside)
        def _():
            c.start()

        edge_sends.append((inside, c))

    for part in range(PARTS):
        hop(shock_ref.at[rows_of(part), lanes(owner)], me + 1, 0, me, part)
        hop(shock_ref.at[rows_of(part), lanes(owner)], me - 1, n_path, me, part)

    def spread(k):
        q = order[k]
        for part in range(PARTS):
            mine = moves.at[q, rows_of(part), lanes(owner)]
            copy(mine, mine, a_send.at[k, part], a_recv.at[q, part], device(owner, q)).wait_recv()
            hop(mine, jnp.where(q < me, me + 1, me - 1), k, q, part)
            for j in range(1, n_y):
                go(copy(mine, mine, b_send.at[k, j, part], b_recv.at[q, j, part],
                        device(across(j) * 2 + core, me)))
            go(copy(mine, mine, c_send.at[k, 0, part], c_recv.at[q, 0, part], device(partner, me)))

    def relay(k):
        q = order[k]
        for part in range(PARTS):
            for j in range(1, n_y):
                source = across(n_y - j) * 2 + core
                got = moves.at[q, rows_of(part), lanes(source)]
                copy(got, got, b_send.at[k, j, part], b_recv.at[q, j, part],
                     device(partner, me)).wait_recv()
                go(copy(got, got, c_send.at[k, j, part], c_recv.at[q, j, part],
                        device(partner, me)))

    def gathered(k):
        q = order[k]
        for part in range(PARTS):
            for j in range(n_y):
                got = moves.at[q, rows_of(part), lanes(across(n_y - j) * 2 + 1 - core)]
                copy(got, got, c_send.at[k, j, part], c_recv.at[q, j, part],
                     device(partner, me)).wait_recv()

    tile = trades

    def values(k):
        @pl.loop(0, trades // tile)
        def _(i):
            rows = pl.ds(pl.multiple_of(i * tile, tile), tile)
            block = shock_ref[...] if k == 0 else moves[order[k]]
            out = lax.dot_general(sens[rows, :], block, BY_LANES, preferred_element_type=F32)
            tv[k, rows, :] = (out + base_cols[rows, :]).astype(BF16)

        @pl.loop(0, n_y)
        def _(i):
            rows = pl.ds(pl.multiple_of(i * n_sets, n_sets), n_sets)
            part_sums = jnp.dot(hot[1, rows, :], tv[k], preferred_element_type=F32)
            send1[k, rows, :] = part_sums.astype(BF16)

        go(copy(send1.at[k], recv1.at[k], s1_send.at[k], s1_recv.at[k], device(partner, me)))

    def set_sums(k, yy):
        rows = pl.ds(pl.multiple_of(yy * n_sets, n_sets), n_sets)
        return jnp.dot(hot[0, rows, :], tv[k], preferred_element_type=F32) + recv1[k, rows, :].astype(F32)

    def cross_owner(k):
        copy(send1.at[k], recv1.at[k], s1_send.at[k], s1_recv.at[k], device(partner, me)).wait_recv()
        for j in range(1, n_y):
            send2[k, j - 1] = set_sums(k, across(j)).astype(BF16)
            go(copy(send2.at[k, j - 1], recv2.at[k, j - 1], s2_send.at[k, j - 1],
                    s2_recv.at[k, j - 1], device(across(j) * 2 + core, me)))
        keep2[k] = set_sums(k, y)

    def cross_path(k):
        total = keep2[k]
        for j in range(1, n_y):
            copy(send2.at[k, j - 1], recv2.at[k, j - 1], s2_send.at[k, j - 1],
                 s2_recv.at[k, j - 1], device(partner, me)).wait_recv()
            total = total + recv2[k, j - 1].astype(F32)
        if k == 0:
            acc[...] = total
        else:
            send3[k - 1] = total.astype(BF16)
            go(copy(send3.at[k - 1], recv3.at[me], s3_send.at[k], s3_recv.at[me],
                    device(owner, order[k])))

    place = (owner_ref[...] % 2) * half + (owner_ref[...] // 2) * n_sets + local_ref[...]
    def one_hots(h):
        key = place - jnp.where(core == h, 0, half)

        @pl.loop(0, n_y)
        def _(i):
            row = lax.broadcasted_iota(jnp.int32, (n_sets, trades), 0) + i * n_sets
            hot[h, pl.ds(pl.multiple_of(i * n_sets, n_sets), n_sets), :] = jnp.where(
                row == key, 1.0, 0.0
            ).astype(BF16)

    base_cols[...] = jnp.broadcast_to(base_ref[...], (cols, trades)).T
    spread(1)
    one_hots(1)
    one_hots(0)
    if n_path > 2:
        spread(2)
    floor = jnp.zeros((1, n_sets), F32)
    for a in range(posted_ref.shape[0]):
        floor = jnp.where(cset_ref[...] == a, posted_ref[a], floor)
    floor_cols[...] = jnp.broadcast_to(floor, (cols, n_sets)).T
    load.wait()
    values(0)
    relay(1)
    for k in range(1, n_path + 2):
        if k + 2 < n_path:
            spread(k + 2)
        if k == 1 and n_path > 2:
            relay(2)
        if k < n_path:
            gathered(k)
            values(k)
        if 1 < k < n_path - 1:
            relay(k + 1)
        if k < n_path + 1:
            cross_owner(k - 1)
        if k >= 2:
            cross_path(k - 2)

    lane_step = lax.broadcasted_iota(jnp.int32, (1, cols), 1) % steps
    factor = jnp.zeros((1, cols), F32)
    for s in range(steps):
        factor = jnp.where(lane_step == s, disc_ref[s], factor)
    nets = acc[...]
    for j in range(1, n_path):
        p = along(j)
        got = recv3.at[p]
        copy(got, got, s3_send.at[j], s3_recv.at[p], device(owner, p)).wait_recv()
        nets = nets + recv3[p].astype(F32)
    exposure = factor * jnp.maximum(nets - floor_cols[...], 0.0)

    pick = (
        lax.broadcasted_iota(jnp.int32, (8, cols), 1) % steps
        == lax.broadcasted_iota(jnp.int32, (8, cols), 0)
    ).astype(F32)
    tot[...] = lax.dot_general(
        pick, exposure, BY_LANES, precision=lax.Precision.HIGHEST, preferred_element_type=F32
    )
    for j in range(1, n_path):
        go(copy(tot, recv4.at[me], s4_send.at[j], s4_recv.at[me], device(owner, along(j))))
    exp_ref[...] = exposure
    sums = tot[...]
    for j in range(1, n_path):
        p = along(j)
        copy(tot, recv4.at[p], s4_send.at[j], s4_recv.at[p], device(owner, p)).wait_recv()
        sums = sums + recv4[p]
    mean_ref[...] = (sums / (cols // steps * n_path))[:steps, :]
    for c in open_sends:
        c.wait_send()
    for inside, c in edge_sends:

        @pl.when(inside)
        def _():
            c.wait_send()


def shards(
    sensitivity,
    present_trade_value,
    trade_set_owner,
    trade_local_set,
    shocks,
    collateral_of_set,
    collateral_posted,
    discount,
):
    n_owner, n_path = lax.axis_size("owner"), lax.axis_size("path")
    trades, factors = sensitivity.shape
    steps = shocks.shape[1]
    cols = shocks.shape[0] * steps
    n_sets = collateral_of_set.shape[0]
    n_y = n_owner // 2
    half = n_y * n_sets
    others = max(n_y - 1, 1)
    vmem = pl.BlockSpec(memory_space=pltpu.VMEM)
    smem = pl.BlockSpec(memory_space=pltpu.SMEM)
    dma = pltpu.SemaphoreType.DMA
    exposure, mean = pl.pallas_call(
        functools.partial(kernel, n_owner, n_path, n_sets, steps),
        out_shape=(
            jax.ShapeDtypeStruct((n_sets, cols), F32),
            jax.ShapeDtypeStruct((steps, n_sets), F32),
        ),
        in_specs=[pl.BlockSpec(memory_space=pl.ANY), vmem, vmem, vmem, vmem, vmem, smem, smem],
        out_specs=(vmem, vmem),
        scratch_shapes=[
            pltpu.VMEM((cols, factors), BF16),
            pltpu.VMEM((trades, factors), BF16),
            pltpu.VMEM((n_path, cols, factors), BF16),
            pltpu.VMEM((trades, cols), F32),
            pltpu.VMEM((n_sets, cols), F32),
            pltpu.VMEM((2, half, trades), BF16),
            pltpu.VMEM((n_path, trades, cols), BF16),
            pltpu.VMEM((n_path, half, cols), BF16),
            pltpu.VMEM((n_path, half, cols), BF16),
            pltpu.VMEM((n_path, n_sets, cols), F32),
            pltpu.VMEM((n_path, others, n_sets, cols), BF16),
            pltpu.VMEM((n_path, others, n_sets, cols), BF16),
            pltpu.VMEM((n_sets, cols), F32),
            pltpu.VMEM((n_path - 1, n_sets, cols), BF16),
            pltpu.VMEM((n_path, n_sets, cols), BF16),
            pltpu.VMEM((8, n_sets), F32),
            pltpu.VMEM((n_path, 8, n_sets), F32),
            dma,
            dma((n_path + 1, PARTS)), dma((n_path, PARTS)),
            dma((n_path, n_y, PARTS)), dma((n_path, n_y, PARTS)),
            dma((n_path, n_y, PARTS)), dma((n_path, n_y, PARTS)),
            dma((n_path,)), dma((n_path,)),
            dma((n_path, others)), dma((n_path, others)),
            dma((n_path,)), dma((n_path,)),
            dma((n_path,)), dma((n_path,)),
        ],
        compiler_params=pltpu.CompilerParams(
            collective_id=0, has_side_effects=True, vmem_limit_bytes=60 * 1024 * 1024
        ),
        cost_estimate=pl.CostEstimate(
            flops=2 * trades * cols * n_path * (factors + 2 * half),
            bytes_accessed=2 * trades * factors,
            transcendentals=0,
        ),
    )(
        sensitivity,
        shocks,
        present_trade_value.reshape(1, trades),
        trade_set_owner.reshape(1, trades),
        trade_local_set.reshape(1, trades),
        collateral_of_set.reshape(1, n_sets),
        collateral_posted,
        discount,
    )
    return exposure, mean.T


def solution(mesh):
    in_specs = (
        P(("groups", "owner", "path"), None),
        P(("groups", "owner", "path")),
        P(("groups", "owner", "path"), None),
        P(("groups", "owner", "path")),
        P(("groups", "path"), None, None),
        P(("groups", "owner")),
        P("groups"),
        P("groups"),
    )
    out_specs = (P(("groups", "owner"), "path"), P(("groups", "owner"), None))
    return jax.shard_map(shards, mesh=mesh, in_specs=in_specs, out_specs=out_specs, check_vma=False)
```
